256 devices in a mesh: group: 8 (over x, z_lo), member: 32 (over y, z_hi, core).
Axes of the slice: x: 4, y: 4, z: 8 (z_hi: 4, z_lo: 2; z = z_hi * 2 + z_lo), core: 2. Of those that a mesh axis runs over, the one named last changes fastest.
Arguments:
- tokens: bfloat16 [2048, 2048], P(('group', 'member')), may hold values from -6 to 6
- expert_ids: int32 [2048, 8], P('group'), may hold values from 0 to 127, all different within a row
- combine: float32 [2048, 8], P('group'), may hold values from 0.05 to 0.5
- hot_group: int32 [16], replicated, may hold values from 0 to 7
- expert_weights: bfloat16 [256, 2048, 1152], P(('group', 'member')), may hold values from -0.1875 to 0.1875
- out_grad: bfloat16 [2048, 2048], P(('group', 'member')), may hold values from -6 to 6
Outputs:
- mixed_out: bfloat16 [2048, 2048], P(('group', 'member'))
- token_grad: bfloat16 [2048, 2048], P(('group', 'member'))
- weight_grad: bfloat16 [256, 2048, 1152], P(('group', 'member'))
The draws below stay inside these ranges and needn't reach their ends.
Inputs may be any that keep to these rules, and one draw needn't show every extreme that they name: `expert_ids`: each row names 8 different experts. `hot_group`: entry j names the group whose expert number j + 16 * group is hot.
All inputs are finite; a program needn't handle non-finite values.
Results may differ from the reference program's by a relative error of at most 0.018.
Values may be sent and summed in bfloat16 or wider, within the bound.
A program may use at most 128 MiB of HBM per device.

```python
import math
import jax
import jax.numpy as jnp
from jax import lax

D = 2048
HALF = 384
TOP = 8
TOK_DEV = 8
EXP_GROUP = 16
EXPERTS = 128
EXPERT_HALVES = 256
TOKENS = 2048
CAP = 24
HOT_CAP = 48
N_GROUP = 8
N_MEMBER = 32


def set_ends(entries, stream_key, smallest, top_value):
    spot = [jax.random.randint(jax.random.fold_in(stream_key, axis), (), 0, length) for axis, length in enumerate(entries.shape)]
    main_axis = entries.shape.index(max(entries.shape))
    next_to = spot[:main_axis] + [(spot[main_axis] + 1) % entries.shape[main_axis]] + spot[main_axis + 1:]
    return entries.at[tuple(spot)].set(smallest).at[tuple(next_to)].set(top_value)


def steps_of(own_key, dims, cuts, smallest, high):
    factor_of, own = 1.0, jax.random.fold_in(own_key, 6)
    for position, shards_of in cuts:
        heights = jnp.exp(jax.random.uniform(jax.random.fold_in(own, position), (shards_of,), jnp.float32, smallest / len(cuts), high / len(cuts)))
        factor_of = factor_of * jnp.repeat(heights, dims[position] // shards_of).reshape([-1 if axis == position else 1 for axis in range(len(dims))])
    return factor_of


def distinct(rng, rows, number_of, top, lift):
    sequence = jax.random.permutation(jax.random.fold_in(rng, 1), number_of)
    pull = sequence
    for power in range(3):
        pull = pull * pull // number_of
    pull = pull * lift // number_of
    tickets = jax.random.randint(jax.random.fold_in(rng, 2), (rows, number_of), 0, 4096) + pull
    holders = jax.random.permutation(jax.random.fold_in(rng, 3), rows)[jnp.arange(number_of) % rows]
    tickets = jnp.where(jnp.arange(rows)[:, None] == holders[None, :], 1 << 14, tickets)
    score = tickets * number_of + jnp.arange(number_of)
    return lax.top_k(score.astype(jnp.int32), top)[1].astype(jnp.int32)


def bell_draw(key, dims, scale, bound, pieces=(), kind=jnp.bfloat16):
    gain = steps_of(key, dims, pieces, -0.22, 0.18) if pieces else 1.0
    entries = jax.random.normal(key, dims, jnp.float32) * scale * gain
    return jnp.minimum(jnp.maximum(entries, -bound), bound).astype(kind)


def setup_inputs(seed: int = 0) -> dict:
    arg_keys = jax.random.split(jax.random.key(seed), 7)
    tokens = bell_draw(arg_keys[0], (TOKENS, D), 1.0, 6.0, ((0, 256),))
    expert_ids = distinct(arg_keys[1], TOKENS, EXPERTS, TOP, 1024)
    combine = jnp.clip(jnp.exp(math.log(0.5) - 2.3025851 * jax.random.uniform(arg_keys[2], (TOKENS, TOP), jnp.float32) ** steps_of(arg_keys[2], (TOKENS, TOP), ((0, 8),), -0.2, 0.2)), 0.05, 0.5)
    hot_group = set_ends(jax.random.randint(arg_keys[3], (EXP_GROUP,), 0, N_GROUP), jax.random.fold_in(arg_keys[3], 1), 0, N_GROUP - 1).astype(jnp.int32)
    expert_weights = bell_draw(arg_keys[4], (EXPERT_HALVES, D, 3 * HALF), (D // 2) ** -0.5, 0.1875, ((0, 256),))
    out_grad = bell_draw(arg_keys[5], (TOKENS, D), 1.0, 6.0, ((0, 256),))
    return dict(tokens=tokens, expert_ids=expert_ids, combine=combine, hot_group=hot_group, expert_weights=expert_weights, out_grad=out_grad)


def expert_pass(rows_in, grad_rows, weights):
    half_width = weights.shape[1] // 3
    pre_act = jnp.dot(rows_in, weights[:, :2 * half_width], preferred_element_type=jnp.float32)
    gate_pre = pre_act[:, :half_width]
    up_pre = pre_act[:, half_width:]
    sigmoid_gate = jax.nn.sigmoid(gate_pre)
    active = gate_pre * sigmoid_gate
    hidden = (active * up_pre).astype(jnp.bfloat16)
    down_w = weights[:, 2 * half_width:]
    partial_value = lax.dot_general(hidden, down_w, (((1,), (1,)), ((), ())), preferred_element_type=jnp.float32).astype(jnp.bfloat16)
    d_hidden = jnp.dot(grad_rows, down_w, preferred_element_type=jnp.float32)
    d_gate = d_hidden * up_pre * sigmoid_gate * (1.0 + gate_pre * (1.0 - sigmoid_gate))
    d_up = d_hidden * active
    d_both = jnp.concatenate([d_gate, d_up], axis=1).astype(jnp.bfloat16)
    d_rows = lax.dot_general(d_both, weights[:, :2 * half_width], (((1,), (1,)), ((), ())), preferred_element_type=jnp.float32).astype(jnp.bfloat16)
    grad_in = lax.dot_general(rows_in, d_both, (((0,), (0,)), ((), ())), preferred_element_type=jnp.float32)
    grad_out = lax.dot_general(grad_rows, hidden, (((0,), (0,)), ((), ())), preferred_element_type=jnp.float32)
    return partial_value, d_rows, jnp.concatenate([grad_in, grad_out], axis=1)


def reference(tokens, expert_ids, combine, hot_group, expert_weights, out_grad):
    group_len = TOK_DEV * N_MEMBER
    expert_range = jnp.arange(EXPERTS, dtype=jnp.int32)
    chosen = expert_ids[:, :, None] == expert_range
    hit_count = jnp.sum(chosen.astype(jnp.int32), axis=1)
    weight = jnp.sum(jnp.where(chosen, combine[:, :, None], jnp.zeros((), jnp.float32)), axis=1)
    group_hits = hit_count.reshape(N_GROUP, group_len, EXPERTS)
    rank_table = jnp.cumsum(group_hits, axis=1) - group_hits
    hot_flag = hot_group[expert_range % EXP_GROUP] == expert_range // EXP_GROUP
    cap_limit = jnp.where(hot_flag, HOT_CAP, CAP)
    kept_slot = (group_hits > 0) & (rank_table < cap_limit)
    hot_ids = (hot_group * EXP_GROUP + jnp.arange(EXP_GROUP, dtype=jnp.int32)).astype(jnp.int32)
    cold_ids = jnp.argsort(hot_flag.astype(jnp.int32), stable=True)[:EXPERTS - EXP_GROUP].astype(jnp.int32)
    offsets = (jnp.arange(N_GROUP, dtype=jnp.int32)[:, None, None] * group_len
               + jnp.arange(group_len, dtype=jnp.int32)[None, None, :])

    def one_expert(running, expert, capacity):
        mixed_term, grad_term, grad_table = running
        kept_e = kept_slot[:, :, expert]
        rank_e = rank_table[:, :, expert]
        slot_range = jnp.arange(capacity, dtype=jnp.int32)
        slot_match = kept_e[:, None, :] & (rank_e[:, None, :] == slot_range[None, :, None])
        token_at = jnp.sum(jnp.where(slot_match, offsets, 0), axis=2).astype(jnp.int32)
        row_live = jnp.any(slot_match, axis=2)
        coeff_used = jnp.where(row_live, weight[token_at, expert], jnp.zeros((), jnp.float32))
        row_block = jnp.where(row_live[..., None], tokens[token_at], jnp.zeros((), jnp.bfloat16))
        grad_rows = (coeff_used[..., None] * out_grad[token_at].astype(jnp.float32)).astype(jnp.bfloat16)
        is_hot = hot_flag[expert]
        flat_tokens = token_at.reshape(-1)
        live_ones = jnp.where(row_live.reshape(-1), 1.0, 0.0).astype(jnp.float32)
        for half_index in range(2):
            layer_w = expert_weights[2 * expert + half_index]
            part, back, block_grad = jax.vmap(expert_pass, in_axes=(0, 0, None))(row_block, grad_rows, layer_w)
            mixed_term = mixed_term.at[flat_tokens].add(coeff_used.reshape(-1)[:, None] * part.reshape(-1, D).astype(jnp.float32))
            grad_term = grad_term.at[flat_tokens].add(live_ones[:, None] * back.reshape(-1, D).astype(jnp.float32))
            rounded = jnp.sum(lax.optimization_barrier(block_grad.astype(jnp.bfloat16)).astype(jnp.float32), axis=0)
            grad_total = jnp.where(is_hot, rounded, jnp.sum(block_grad, axis=0))
            grad_table = grad_table.at[2 * expert + half_index].set(grad_total.astype(jnp.bfloat16))
        return (mixed_term, grad_term, grad_table), None

    start = (jnp.zeros((TOKENS, D), jnp.float32), jnp.zeros((TOKENS, D), jnp.float32),
             jnp.zeros(expert_weights.shape, jnp.bfloat16))
    running, _ = lax.scan(lambda state_now, expert: one_expert(state_now, expert, CAP), start, cold_ids)
    running, _ = lax.scan(lambda state_now, expert: one_expert(state_now, expert, HOT_CAP), running, hot_ids)
    mixed_term, grad_term, grad_table = running
    return mixed_term.astype(jnp.bfloat16), grad_term.astype(jnp.bfloat16), grad_table
```

```python
import functools

import jax
import jax.numpy as jnp
from jax import lax
from jax.experimental import pallas as pl
from jax.experimental.pallas import tpu as pltpu
from jax.sharding import PartitionSpec as P

MESH = pl.DeviceIdType.MESH
F32 = jnp.float32
BF16 = jnp.bfloat16
CAP = 24
HOT_CAP = 48
CHUNKS = 4


def wait(ref, sem):
    pltpu.make_async_copy(ref, ref, sem).wait()


def dot(a, b, dims):
    return lax.dot_general(a, b, (dims, ((), ())), preferred_element_type=F32)


def layer(
    groups, ny, nz,
    hot_ref, table_ref, tok_ref, grad_ref, w_hbm,
    out_ref, wg_hbm,
    w, buf, send, rows, pick, scale, spread, acc, hid, dab,
    pair, other, total, ret, res, yrecv, ysum, zrecv, fin, wg,
    w_sem, z_send, z_recv, y_send, y_recv, g_send, g_recv, f_send, f_recv,
    h_send, h_recv, r_send, r_recv, ry_send, ry_recv, rz_send, rz_recv,
    o_send, o_recv, wg_sem,
):
    chunks, _, _, width = buf.shape
    tokens = table_ref.shape[1]
    top = table_ref.shape[0] // 2
    slots = groups * HOT_CAP
    half = hid.shape[1]
    my_group = lax.axis_index("group")
    member = lax.axis_index("member")
    core = member % 2
    local = member // 2
    z = local % nz
    y = local // nz
    partner = (my_group, member + 1 - 2 * core)

    def z_peer(step, kind):
        return (my_group, (y * nz + (z + step) % nz) * 2 + kind)

    def y_peer(step):
        return (my_group, (((y + step) % ny) * nz + z) * 2 + core)

    def g_peer(step):
        return ((my_group + step) % groups, member)

    w_copy = pltpu.make_async_copy(w_hbm.at[0], w, w_sem)
    w_copy.start()

    barrier = pltpu.get_barrier_semaphore()
    peers = [partner]
    peers += [z_peer(s, k) for s in range(1, nz) for k in range(2)]
    peers += [y_peer(s) for s in range(1, ny)]
    peers += [g_peer(s) for s in range(1, groups)]
    for peer in peers:
        pl.semaphore_signal(barrier, inc=1, device_id=peer, device_id_type=MESH)
    pl.semaphore_wait(barrier, len(peers))

    def push(src, dst, send_sem, recv_sem, peer):
        pltpu.make_async_remote_copy(
            src_ref=src, dst_ref=dst, send_sem=send_sem, recv_sem=recv_sem,
            device_id=peer, device_id_type=MESH,
        ).start()

    for ch in range(chunks):
        cols = pl.ds(ch * width, width)
        place = buf.at[ch, member]
        sources = (tok_ref.at[:, cols], grad_ref.at[:, cols])
        for step in range(1, nz):
            for kind in range(2):
                push(sources[kind], place, z_send.at[ch], z_recv.at[ch], z_peer(step, kind))
        for kind in range(2):

            @pl.when(core == kind)
            def _():
                pltpu.make_async_copy(sources[kind], place, z_recv.at[ch]).start()
                push(sources[1 - kind], place, z_send.at[ch], z_recv.at[ch], partner)

    ids = table_ref[0:top, :]
    weights = table_ref[top : 2 * top, :]
    group_row = lax.broadcasted_iota(jnp.int32, (groups, tokens), 0)
    wanted = (group_row * (ny * nz) + local).astype(F32)
    hit = jnp.zeros((groups, tokens), F32)
    weight = jnp.zeros((groups, tokens), F32)
    for k in range(top):
        match = ids[k : k + 1, :] == wanted
        hit = hit + jnp.where(match, 1.0, 0.0)
        weight = weight + jnp.where(match, weights[k : k + 1, :], 0.0)
    before = lax.broadcasted_iota(jnp.int32, (tokens, tokens), 0) < lax.broadcasted_iota(
        jnp.int32, (tokens, tokens), 1
    )
    earlier = jnp.where(before, 1.0, 0.0).astype(BF16)
    rank = dot(hit.astype(BF16), earlier, ((1,), (0,)))
    limit = jnp.where(group_row == hot_ref[local], float(HOT_CAP), float(CAP))
    kept = (hit > 0.0) & (rank < limit)
    rank = jnp.where(kept, rank, -1.0)
    is_rows = core == 0
    gather_weight = jnp.where(is_rows, 1.0, weight)
    spread_weight = jnp.where(is_rows, weight, 1.0)
    slot = lax.broadcasted_iota(jnp.int32, (HOT_CAP, tokens), 0).astype(F32)
    for g in range(groups):
        at = pl.ds(g * HOT_CAP, HOT_CAP)
        one = jnp.where(rank[g : g + 1, :] == slot, 1.0, 0.0)
        pick[at, :] = one.astype(BF16)
        scale[at, :] = jnp.broadcast_to(
            jnp.sum(one * gather_weight[g : g + 1, :], axis=1, keepdims=True), (HOT_CAP, 128)
        )
        acc[at, 0:tokens] = one * spread_weight[g : g + 1, :]
    turned = acc[:, 0:tokens].T
    spread[0] = turned.astype(BF16)
    spread[1] = (turned - turned.astype(BF16).astype(F32)).astype(BF16)

    def to_y(ch):
        mine = pl.ds(y * nz * 2, nz * 2)
        wait(buf.at[ch, mine], z_recv.at[ch])
        for step in range(1, ny):
            push(buf.at[ch, mine], buf.at[ch, mine], y_send.at[ch], y_recv.at[ch], y_peer(step))

    def to_owner(ch):
        wait(buf.at[ch, pl.ds(0, (ny - 1) * nz * 2)], y_recv.at[ch])
        block = buf[ch].astype(F32).reshape(tokens, width).astype(BF16)
        picked = dot(pick[...], block, ((1,), (0,))) * scale[:, 0:1]
        send[ch] = picked.astype(BF16).reshape(groups, HOT_CAP, width)
        for step in range(1, groups):
            peer = g_peer(step)
            push(send.at[ch, peer[0]], rows.at[core, ch, my_group], g_send.at[ch], g_recv.at[ch], peer)
        pltpu.make_async_copy(
            send.at[ch, my_group], rows.at[core, ch, my_group], g_recv.at[ch]
        ).start()

    def to_partner(ch):
        wait(rows.at[core, ch], g_recv.at[ch])
        push(rows.at[core, ch], rows.at[core, ch], f_send.at[ch], f_recv.at[ch], partner)

    def accumulate(ch):
        wait(rows.at[1 - core, ch], f_recv.at[ch])
        if ch == 0:
            w_copy.wait()
        at = pl.ds(ch * width, width)
        pre = dot(rows[0, ch].reshape(slots, width), w[at, 0 : 2 * half], ((1,), (0,)))
        down = dot(rows[1, ch].reshape(slots, width), w[at, 2 * half :], ((1,), (0,)))
        if ch == 0:
            acc[:, 0 : 2 * half] = pre
            acc[:, 2 * half :] = down
        else:
            acc[:, 0 : 2 * half] += pre
            acc[:, 2 * half :] += down

    for step in range(chunks + 3):
        for lag, phase in enumerate((to_y, to_owner, to_partner, accumulate)):
            if 0 <= step - lag < chunks:
                phase(step - lag)

    @pl.loop(0, groups)
    def _(g):
        at = pl.ds(pl.multiple_of(g * HOT_CAP, HOT_CAP), HOT_CAP)
        gate = acc[at, 0:half]
        up = acc[at, half : 2 * half]
        d_hidden = acc[at, 2 * half :]
        sig = jax.nn.sigmoid(gate)
        active = gate * sig
        hid[at, :] = (active * up).astype(BF16)
        dab[at, 0:half] = (d_hidden * up * sig * (1.0 + gate * (1.0 - sig))).astype(BF16)
        dab[at, half:] = (d_hidden * active).astype(BF16)

    def results(ch):
        at = pl.ds(ch * width, width)
        part = dot(hid[...], w[at, 2 * half :], ((1,), (1,)))
        back = dot(dab[...], w[at, 0 : 2 * half], ((1,), (1,)))
        pair[0, ch] = part.astype(BF16).reshape(groups, HOT_CAP, width)
        pair[1, ch] = back.astype(BF16).reshape(groups, HOT_CAP, width)
        push(pair.at[1 - core, ch], other.at[ch], h_send.at[ch], h_recv.at[ch], partner)

    def to_origin(ch):
        wait(other.at[ch], h_recv.at[ch])
        total[ch] = (pair[core, ch].astype(F32) + other[ch].astype(F32)).astype(BF16)
        for step in range(1, groups):
            peer = g_peer(step)
            push(total.at[ch, peer[0]], ret.at[ch, my_group], r_send.at[ch], r_recv.at[ch], peer)
        pltpu.make_async_copy(total.at[ch, my_group], ret.at[ch, my_group], r_recv.at[ch]).start()

    def weight_part(ch):
        at = pl.ds(ch * width, width)
        wg[at, 0 : 2 * half] = dot(
            rows[0, ch].reshape(slots, width), dab[...], ((0,), (0,))
        ).astype(BF16)
        wg[at, 2 * half :] = dot(
            rows[1, ch].reshape(slots, width), hid[...], ((0,), (0,))
        ).astype(BF16)
        pltpu.make_async_copy(wg.at[at], wg_hbm.at[0, at], wg_sem.at[ch]).start()

    def back_y(ch):
        wait(ret.at[ch], r_recv.at[ch])
        got = ret[ch].reshape(slots, width)
        mixed = dot(spread[0], got, ((1,), (0,))) + dot(spread[1], got, ((1,), (0,)))
        res[ch] = mixed.astype(BF16).reshape(ny, nz, 16, width)
        for step in range(1, ny):
            push(
                res.at[ch, (y + step) % ny], yrecv.at[ch, y], ry_send.at[ch], ry_recv.at[ch],
                y_peer(step),
            )
        pltpu.make_async_copy(res.at[ch, y], yrecv.at[ch, y], ry_recv.at[ch]).start()

    def back_z(ch):
        wait(yrecv.at[ch], ry_recv.at[ch])
        ysum[ch] = jnp.sum(yrecv[ch].astype(F32), axis=0).astype(BF16)
        for step in range(1, nz):
            push(
                ysum.at[ch, (z + step) % nz], zrecv.at[ch, z], rz_send.at[ch], rz_recv.at[ch],
                z_peer(step, core),
            )
        pltpu.make_async_copy(ysum.at[ch, z], zrecv.at[ch, z], rz_recv.at[ch]).start()

    def finish(ch):
        wait(zrecv.at[ch], rz_recv.at[ch])
        done = jnp.sum(zrecv[ch].astype(F32), axis=0)
        fin[ch] = done.reshape(2, 8, width).astype(BF16)
        place = out_ref.at[core, ch]
        push(fin.at[ch, 1 - core], place, o_send.at[ch], o_recv.at[ch], partner)
        pltpu.make_async_copy(fin.at[ch, core], place, o_recv.at[ch]).start()

    phases = (results, to_origin, weight_part, back_y, back_z, finish)
    for step in range(chunks + len(phases) - 1):
        for lag, phase in enumerate(phases):
            if 0 <= step - lag < chunks:
                phase(step - lag)

    for ch in range(chunks):
        at = pl.ds(ch * width, width)
        pltpu.make_async_copy(wg.at[at], wg_hbm.at[0, at], wg_sem.at[ch]).wait()
        wait(buf.at[ch, pl.ds(0, 2 * nz - 1)], z_send.at[ch])
        wait(buf.at[ch, pl.ds(0, (ny - 1) * nz * 2)], y_send.at[ch])
        wait(send.at[ch, pl.ds(0, groups - 1)], g_send.at[ch])
        wait(rows.at[core, ch], f_send.at[ch])
        wait(pair.at[1 - core, ch], h_send.at[ch])
        wait(total.at[ch, pl.ds(0, groups - 1)], r_send.at[ch])
        wait(res.at[ch, pl.ds(0, ny - 1)], ry_send.at[ch])
        wait(ysum.at[ch, pl.ds(0, nz - 1)], rz_send.at[ch])
        wait(fin.at[ch, 1 - core], o_send.at[ch])
        wait(fin.at[ch], o_recv.at[ch])


def shards(ny, nz, tokens, expert_ids, combine, hot_group, expert_weights, out_grad):
    groups = lax.axis_size("group")
    chips = ny * nz
    rows_here, model_width = tokens.shape
    group_len = expert_ids.shape[0]
    hidden3 = expert_weights.shape[2]
    half = hidden3 // 3
    width = model_width // CHUNKS
    slots = groups * HOT_CAP
    table = jnp.concatenate([expert_ids.astype(F32).T, combine.T], axis=0)
    dma = pltpu.SemaphoreType.DMA
    block = (CHUNKS, groups, HOT_CAP, width)
    any_space = pl.BlockSpec(memory_space=pl.ANY)
    out, weight_grad = pl.pallas_call(
        functools.partial(layer, groups, ny, nz),
        out_shape=(
            jax.ShapeDtypeStruct((2, CHUNKS, rows_here, width), BF16),
            jax.ShapeDtypeStruct(expert_weights.shape, BF16),
        ),
        in_specs=[
            pl.BlockSpec(memory_space=pltpu.SMEM),
            pl.BlockSpec(memory_space=pltpu.VMEM),
            any_space,
            any_space,
            any_space,
        ],
        out_specs=(pl.BlockSpec(memory_space=pltpu.VMEM), any_space),
        scratch_shapes=[
            pltpu.VMEM((model_width, hidden3), BF16),
            pltpu.VMEM((CHUNKS, 2 * chips, rows_here, width), BF16),
            pltpu.VMEM(block, BF16),
            pltpu.VMEM((2,) + block, BF16),
            pltpu.VMEM((slots, group_len), BF16),
            pltpu.VMEM((slots, 128), F32),
            pltpu.VMEM((2, group_len, slots), BF16),
            pltpu.VMEM((slots, hidden3), F32),
            pltpu.VMEM((slots, half), BF16),
            pltpu.VMEM((slots, 2 * half), BF16),
            pltpu.VMEM((2,) + block, BF16),
            pltpu.VMEM(block, BF16),
            pltpu.VMEM(block, BF16),
            pltpu.VMEM(block, BF16),
            pltpu.VMEM((CHUNKS, ny, nz, 16, width), BF16),
            pltpu.VMEM((CHUNKS, ny, nz, 16, width), BF16),
            pltpu.VMEM((CHUNKS, nz, 16, width), BF16),
            pltpu.VMEM((CHUNKS, nz, 16, width), BF16),
            pltpu.VMEM((CHUNKS, 2, rows_here, width), BF16),
            pltpu.VMEM((model_width, hidden3), BF16),
            dma,
        ]
        + [dma((CHUNKS,))] * 19,
        compiler_params=pltpu.CompilerParams(
            collective_id=0, has_side_effects=True, vmem_limit_bytes=56 * 2**20
        ),
        cost_estimate=pl.CostEstimate(
            flops=6 * slots * model_width * hidden3, bytes_accessed=4 * model_width * hidden3,
            transcendentals=slots * half,
        ),
    )(hot_group, table, tokens, out_grad, expert_weights)
    out = out.transpose(0, 2, 1, 3).reshape(2, rows_here, model_width)
    return out[0], out[1], weight_grad


def solution(mesh):
    nz = 4 if mesh.shape["member"] == 32 else 2
    ny = mesh.shape["member"] // (2 * nz)
    return jax.shard_map(
        functools.partial(shards, ny, nz),
        mesh=mesh,
        in_specs=(
            P(("group", "member"), None),
            P("group", None),
            P("group", None),
            P(),
            P(("group", "member"), None, None),
            P(("group", "member"), None),
        ),
        out_specs=(
            P(("group", "member"), None),
            P(("group", "member"), None),
            P(("group", "member"), None, None),
        ),
        check_vma=False,
    )
```

```python
import functools

import jax
import jax.numpy as jnp
from jax import lax
from jax.experimental import pallas as pl
from jax.experimental.pallas import tpu as pltpu
from jax.sharding import PartitionSpec as P

MESH = pl.DeviceIdType.MESH
F32 = jnp.float32
BF16 = jnp.bfloat16
CAP = 24
HOT_CAP = 48
VMEM_BYTES = 56 * 2**20
Z_CUTS = (256, 512, 1280)
IN_CUTS = (256, 512, 768, 512)
OUT_CUTS = (256, 512, 512, 512, 256)


def spans(cuts, width):
    whole = sum(cuts)
    ends = [sum(cuts[: i + 1]) * width // whole for i in range(len(cuts))]
    return [(a, b) for a, b in zip([0] + ends[:-1], ends)]


def wait(ref, sem):
    pltpu.make_async_copy(ref, ref, sem).wait()


def dot(a, b, dims):
    return lax.dot_general(a, b, (dims, ((), ())), preferred_element_type=F32)


def layer(
    groups, ny, nz,
    hot_ref, ids_ref, weights_ref, tok_ref, grad_ref, w_hbm,
    out_ref, wg,
    w, buf, send, rows, pick, scale, spread, acc, hid, dab,
    pair, other, total, ret, res, yrecv, ysum, zrecv, fin,
    w_sem, z_send, z_recv, y_send, y_recv, g_send, g_recv, f_send, f_recv,
    h_send, h_recv, r_send, r_recv, ry_send, ry_recv, rz_send, rz_recv,
    o_send, o_recv,
):
    model_width = tok_ref.shape[1]
    z_spans = spans(Z_CUTS, model_width)
    in_spans = spans(IN_CUTS, model_width)
    out_spans = spans(OUT_CUTS, model_width)
    top, tokens = ids_ref.shape
    slots = groups * HOT_CAP
    half = hid.shape[1]
    my_group = lax.axis_index("group")
    member = lax.axis_index("member")
    core = member % 2
    local = member // 2
    z = local % nz
    y = local // nz
    partner = (my_group, member + 1 - 2 * core)

    def z_peer(step, kind):
        return (my_group, (y * nz + (z + step) % nz) * 2 + kind)

    def y_peer(step):
        return (my_group, (((y + step) % ny) * nz + z) * 2 + core)

    def g_peer(step):
        return ((my_group + step) % groups, member)

    w_copy = pltpu.make_async_copy(w_hbm.at[0], w, w_sem)
    w_copy.start()

    barrier = pltpu.get_barrier_semaphore()
    peers = [partner]
    peers += [z_peer(s, k) for s in range(1, nz) for k in range(2)]
    peers += [y_peer(s) for s in range(1, ny)]
    peers += [g_peer(s) for s in range(1, groups)]
    for peer in peers:
        pl.semaphore_signal(barrier, inc=1, device_id=peer, device_id_type=MESH)
    pl.semaphore_wait(barrier, len(peers))

    def push(src, dst, send_sem, recv_sem, peer):
        pltpu.make_async_remote_copy(
            src_ref=src, dst_ref=dst, send_sem=send_sem, recv_sem=recv_sem,
            device_id=peer, device_id_type=MESH,
        ).start()

    def columns(span):
        return pl.ds(span[0], span[1] - span[0])

    for ch, span in enumerate(z_spans):
        cols = columns(span)
        place = buf.at[member, :, cols]
        sources = (tok_ref.at[:, cols], grad_ref.at[:, cols])
        for step in range(1, nz):
            for kind in range(2):
                push(sources[kind], place, z_send.at[ch], z_recv.at[ch], z_peer(step, kind))
        for kind in range(2):

            @pl.when(core == kind)
            def _():
                pltpu.make_async_copy(sources[kind], place, z_recv.at[ch]).start()
                push(sources[1 - kind], place, z_send.at[ch], z_recv.at[ch], partner)

    ids = ids_ref[...]
    weights = weights_ref[...]
    group_row = lax.broadcasted_iota(jnp.int32, (groups, tokens), 0)
    wanted = group_row * (ny * nz) + local
    hit = jnp.zeros((groups, tokens), F32)
    weight = jnp.zeros((groups, tokens), F32)
    for k in range(top):
        match = ids[k : k + 1, :] == wanted
        hit = hit + jnp.where(match, 1.0, 0.0)
        weight = weight + jnp.where(match, weights[k : k + 1, :], 0.0)
    before = lax.broadcasted_iota(jnp.int32, (tokens, tokens), 0) < lax.broadcasted_iota(
        jnp.int32, (tokens, tokens), 1
    )
    earlier = jnp.where(before, 1.0, 0.0).astype(BF16)
    rank = dot(hit.astype(BF16), earlier, ((1,), (0,)))
    limit = jnp.where(group_row == hot_ref[local], float(HOT_CAP), float(CAP))
    kept = (hit > 0.0) & (rank < limit)
    rank = jnp.where(kept, rank, -1.0)
    is_rows = core == 0
    gather_weight = jnp.where(is_rows, 1.0, weight)
    spread_weight = jnp.where(is_rows, weight, 1.0)
    slot = lax.broadcasted_iota(jnp.int32, (HOT_CAP, tokens), 0).astype(F32)
    for g in range(groups):
        at = pl.ds(g * HOT_CAP, HOT_CAP)
        one = jnp.where(rank[g : g + 1, :] == slot, 1.0, 0.0)
        pick[at, :] = one.astype(BF16)
        scale[at, :] = jnp.broadcast_to(
            jnp.sum(one * gather_weight[g : g + 1, :], axis=1, keepdims=True), (HOT_CAP, 128)
        )
        acc[at, 0:tokens] = one * spread_weight[g : g + 1, :]
    turned = acc[:, 0:tokens].T
    spread[0] = turned.astype(BF16)
    spread[1] = (turned - turned.astype(BF16).astype(F32)).astype(BF16)

    def to_y(ch):
        mine = pl.ds(y * nz * 2, nz * 2)
        first, last = in_spans[ch]
        for zc, (a, b) in enumerate(z_spans):
            if first < b <= last or (a < last <= b and b > last):
                if zc not in z_done:
                    z_done.append(zc)
                    wait(buf.at[mine, :, columns((a, b))], z_recv.at[zc])
        block = buf.at[mine, :, columns(in_spans[ch])]
        for step in range(1, ny):
            push(block, block, y_send.at[ch], y_recv.at[ch], y_peer(step))

    def to_owner(ch):
        cols = columns(in_spans[ch])
        wait(buf.at[pl.ds(0, (ny - 1) * nz * 2), :, cols], y_recv.at[ch])
        width = cols.size
        block = buf[:, :, cols].astype(F32).reshape(tokens, width).astype(BF16)
        picked = dot(pick[...], block, ((1,), (0,))) * scale[:, 0:1]
        send[:, :, cols] = picked.astype(BF16).reshape(groups, HOT_CAP, width)
        place = rows.at[core, my_group, :, cols]
        for step in range(1, groups):
            peer = g_peer(step)
            push(send.at[peer[0], :, cols], place, g_send.at[ch], g_recv.at[ch], peer)
        pltpu.make_async_copy(send.at[my_group, :, cols], place, g_recv.at[ch]).start()

    def to_partner(ch):
        block = rows.at[core, :, :, columns(in_spans[ch])]
        wait(block, g_recv.at[ch])
        push(block, block, f_send.at[ch], f_recv.at[ch], partner)

    def accumulate(ch):
        at = columns(in_spans[ch])
        wait(rows.at[1 - core, :, :, at], f_recv.at[ch])
        if ch == 0:
            w_copy.wait()
        pre = dot(rows[0, :, :, at].reshape(slots, at.size), w[at, 0 : 2 * half], ((1,), (0,)))
        down = dot(rows[1, :, :, at].reshape(slots, at.size), w[at, 2 * half :], ((1,), (0,)))
        if ch == 0:
            acc[:, 0 : 2 * half] = pre
            acc[:, 2 * half :] = down
        else:
            acc[:, 0 : 2 * half] += pre
            acc[:, 2 * half :] += down

    z_done = []
    chunks = len(in_spans)
    for step in range(chunks + 3):
        for lag, phase in enumerate((to_y, to_owner, to_partner, accumulate)):
            if 0 <= step - lag < chunks:
                phase(step - lag)

    @pl.loop(0, groups)
    def _(g):
        at = pl.ds(pl.multiple_of(g * HOT_CAP, HOT_CAP), HOT_CAP)
        gate = acc[at, 0:half]
        up = acc[at, half : 2 * half]
        d_hidden = acc[at, 2 * half :]
        sig = jax.nn.sigmoid(gate)
        active = gate * sig
        hid[at, :] = (active * up).astype(BF16)
        dab[at, 0:half] = (d_hidden * up * sig * (1.0 + gate * (1.0 - sig))).astype(BF16)
        dab[at, half:] = (d_hidden * active).astype(BF16)

    def results(ch):
        at = columns(out_spans[ch])
        part = dot(hid[...], w[at, 2 * half :], ((1,), (1,)))
        back = dot(dab[...], w[at, 0 : 2 * half], ((1,), (1,)))
        pair[0, :, :, at] = part.astype(BF16).reshape(groups, HOT_CAP, at.size)
        pair[1, :, :, at] = back.astype(BF16).reshape(groups, HOT_CAP, at.size)
        push(pair.at[1 - core, :, :, at], other.at[:, :, at], h_send.at[ch], h_recv.at[ch], partner)

    def to_origin(ch):
        at = columns(out_spans[ch])
        wait(other.at[:, :, at], h_recv.at[ch])
        total[:, :, at] = (pair[core, :, :, at].astype(F32) + other[:, :, at].astype(F32)).astype(BF16)
        place = ret.at[my_group, :, at]
        for step in range(1, groups):
            peer = g_peer(step)
            push(total.at[peer[0], :, at], place, r_send.at[ch], r_recv.at[ch], peer)
        pltpu.make_async_copy(total.at[my_group, :, at], place, r_recv.at[ch]).start()

    def weight_part(ch):
        at = columns(out_spans[ch])
        wg[0, at, 0 : 2 * half] = dot(
            rows[0, :, :, at].reshape(slots, at.size), dab[...], ((0,), (0,))
        ).astype(BF16)
        wg[0, at, 2 * half :] = dot(
            rows[1, :, :, at].reshape(slots, at.size), hid[...], ((0,), (0,))
        ).astype(BF16)

    def back_y(ch):
        at = columns(out_spans[ch])
        wait(ret.at[:, :, at], r_recv.at[ch])
        got = ret[:, :, at].reshape(slots, at.size)
        mixed = dot(spread[0], got, ((1,), (0,))) + dot(spread[1], got, ((1,), (0,)))
        res[:, :, :, at] = mixed.astype(BF16).reshape(ny, nz, 16, at.size)
        place = yrecv.at[y, :, :, at]
        for step in range(1, ny):
            push(
                res.at[(y + step) % ny, :, :, at], place, ry_send.at[ch], ry_recv.at[ch],
                y_peer(step),
            )
        pltpu.make_async_copy(res.at[y, :, :, at], place, ry_recv.at[ch]).start()

    def back_z(ch):
        at = columns(out_spans[ch])
        wait(yrecv.at[:, :, :, at], ry_recv.at[ch])
        ysum[:, :, at] = jnp.sum(yrecv[:, :, :, at].astype(F32), axis=0).astype(BF16)
        place = zrecv.at[z, :, at]
        for step in range(1, nz):
            push(
                ysum.at[(z + step) % nz, :, at], place, rz_send.at[ch], rz_recv.at[ch],
                z_peer(step, core),
            )
        pltpu.make_async_copy(ysum.at[z, :, at], place, rz_recv.at[ch]).start()

    def finish(ch):
        at = columns(out_spans[ch])
        wait(zrecv.at[:, :, at], rz_recv.at[ch])
        done = jnp.sum(zrecv[:, :, at].astype(F32), axis=0)
        fin[:, :, at] = done.reshape(2, 8, at.size).astype(BF16)
        place = out_ref.at[core, :, at]
        push(fin.at[1 - core, :, at], place, o_send.at[ch], o_recv.at[ch], partner)
        pltpu.make_async_copy(fin.at[core, :, at], place, o_recv.at[ch]).start()

    phases = (results, to_origin, weight_part, back_y, back_z, finish)
    chunks = len(out_spans)
    for step in range(chunks + len(phases) - 1):
        for lag, phase in enumerate(phases):
            if 0 <= step - lag < chunks:
                phase(step - lag)

    for ch, span in enumerate(z_spans):
        wait(buf.at[pl.ds(0, 2 * nz - 1), :, columns(span)], z_send.at[ch])
    for ch, span in enumerate(in_spans):
        at = columns(span)
        wait(buf.at[pl.ds(0, (ny - 1) * nz * 2), :, at], y_send.at[ch])
        wait(send.at[pl.ds(0, groups - 1), :, at], g_send.at[ch])
        wait(rows.at[core, :, :, at], f_send.at[ch])
    for ch, span in enumerate(out_spans):
        at = columns(span)
        wait(pair.at[1 - core, :, :, at], h_send.at[ch])
        wait(total.at[pl.ds(0, groups - 1), :, at], r_send.at[ch])
        wait(res.at[pl.ds(0, ny - 1), :, :, at], ry_send.at[ch])
        wait(ysum.at[pl.ds(0, nz - 1), :, at], rz_send.at[ch])
        wait(fin.at[1 - core, :, at], o_send.at[ch])
        wait(fin.at[:, :, at], o_recv.at[ch])


def shards(ny, nz, tokens, expert_ids, combine, hot_group, expert_weights, out_grad):
    groups = lax.axis_size("group")
    chips = ny * nz
    rows_here, model_width = tokens.shape
    group_len = expert_ids.shape[0]
    hidden3 = expert_weights.shape[2]
    half = hidden3 // 3
    slots = groups * HOT_CAP
    dma = pltpu.SemaphoreType.DMA
    block = (groups, HOT_CAP, model_width)
    hbm = pl.BlockSpec(memory_space=pltpu.HBM)
    vmem = pl.BlockSpec(memory_space=pltpu.VMEM)
    n_z, n_in, n_out = len(Z_CUTS), len(IN_CUTS), len(OUT_CUTS)
    out, weight_grad = pl.pallas_call(
        functools.partial(layer, groups, ny, nz),
        out_shape=(
            pltpu.VMEM((2, rows_here, model_width), BF16),
            pltpu.VMEM(expert_weights.shape, BF16),
        ),
        in_specs=[
            pl.BlockSpec(memory_space=pltpu.SMEM), vmem, vmem, hbm, hbm, hbm,
        ],
        out_specs=(vmem, vmem),
        scratch_shapes=[
            pltpu.VMEM((model_width, hidden3), BF16),
            pltpu.VMEM((2 * chips, rows_here, model_width), BF16),
            pltpu.VMEM(block, BF16),
            pltpu.VMEM((2,) + block, BF16),
            pltpu.VMEM((slots, group_len), BF16),
            pltpu.VMEM((slots, 128), F32),
            pltpu.VMEM((2, group_len, slots), BF16),
            pltpu.VMEM((slots, hidden3), F32),
            pltpu.VMEM((slots, half), BF16),
            pltpu.VMEM((slots, 2 * half), BF16),
            pltpu.VMEM((2,) + block, BF16),
            pltpu.VMEM(block, BF16),
            pltpu.VMEM(block, BF16),
            pltpu.VMEM(block, BF16),
            pltpu.VMEM((ny, nz, 16, model_width), BF16),
            pltpu.VMEM((ny, nz, 16, model_width), BF16),
            pltpu.VMEM((nz, 16, model_width), BF16),
            pltpu.VMEM((nz, 16, model_width), BF16),
            pltpu.VMEM((2, rows_here, model_width), BF16),
            dma,
        ]
        + [dma((n_z,))] * 2
        + [dma((n_in,))] * 6
        + [dma((n_out,))] * 10,
        compiler_params=pltpu.CompilerParams(
            collective_id=0, has_side_effects=True, vmem_limit_bytes=VMEM_BYTES
        ),
        cost_estimate=pl.CostEstimate(
            flops=6 * slots * model_width * hidden3, bytes_accessed=4 * model_width * hidden3,
            transcendentals=slots * half,
        ),
    )(hot_group, expert_ids.T, combine.T, tokens, out_grad, expert_weights)
    return out[0], out[1], weight_grad


def solution(mesh):
    nz = 4 if mesh.shape["member"] == 32 else 2
    ny = mesh.shape["member"] // (2 * nz)
    return jax.shard_map(
        functools.partial(shards, ny, nz),
        mesh=mesh,
        in_specs=(
            P(("group", "member"), None),
            P("group", None),
            P("group", None),
            P(),
            P(("group", "member"), None, None),
            P(("group", "member"), None),
        ),
        out_specs=(
            P(("group", "member"), None),
            P(("group", "member"), None),
            P(("group", "member"), None, None),
        ),
        check_vma=False,
    )
```

```python
import functools

import jax
import jax.numpy as jnp
from jax import lax
from jax.experimental import pallas as pl
from jax.experimental.pallas import tpu as pltpu
from jax.sharding import PartitionSpec as P

MESH = pl.DeviceIdType.MESH
F32 = jnp.float32
BF16 = jnp.bfloat16
CAP = 24
HOT_CAP = 48
VMEM_BYTES = 56 * 2**20
Z_CUTS = (512, 512, 1024)
IN_CUTS = (512, 512, 512, 512)
LATE_CUTS = (1024, 1024)
OUT_CUTS = (512, 512, 512, 512)
Y_CUTS = (1024, 512, 512)
FIRST = 32
EARLY = 2


def spans(cuts, width):
    whole = sum(cuts)
    ends = [sum(cuts[: i + 1]) * width // whole for i in range(len(cuts))]
    return [(a, b) for a, b in zip([0] + ends[:-1], ends)]


def wait(ref, sem):
    pltpu.make_async_copy(ref, ref, sem).wait()


def dot(a, b, dims):
    return lax.dot_general(a, b, (dims, ((), ())), preferred_element_type=F32)


def layer(
    groups, ny, nz,
    hot_ref, ids_ref, weights_ref, tok_ref, grad_ref, w_hbm,
    out_ref, wg,
    w, buf, send, rows, pick, scale, spread, acc, hid, dab,
    pair, other, total, ret, res, yrecv, ysum, zrecv, fin,
    w_sem, z_send, z_recv, y_send, y_recv, g_send, g_recv, f_send, f_recv,
    h_send, h_recv, r_send, r_recv, ry_send, ry_recv, rz_send, rz_recv,
    o_send, o_recv,
):
    model_width = tok_ref.shape[1]
    z_spans = spans(Z_CUTS, model_width)
    in_spans = spans(IN_CUTS, model_width)
    late_spans = spans(LATE_CUTS, model_width)
    out_spans = spans(OUT_CUTS, model_width)
    back_spans = spans(Y_CUTS, model_width)
    both = ((0, FIRST), (FIRST, HOT_CAP))
    in_items = [(both[0], span) for span in in_spans] + [(both[1], span) for span in late_spans]
    out_items = [(both[0], span) for span in out_spans[:EARLY]]
    out_items += [(both[1], (0, out_spans[EARLY - 1][1]))]
    out_items += [((0, HOT_CAP), span) for span in out_spans[EARLY:]]
    top, tokens = ids_ref.shape
    slots = groups * HOT_CAP
    half = hid.shape[1]
    my_group = lax.axis_index("group")
    member = lax.axis_index("member")
    core = member % 2
    local = member // 2
    z = local % nz
    y = local // nz
    partner = (my_group, member + 1 - 2 * core)

    def z_peer(step, kind):
        return (my_group, (y * nz + (z + step) % nz) * 2 + kind)

    def y_peer(step):
        return (my_group, (((y + step) % ny) * nz + z) * 2 + core)

    def g_peer(step):
        return ((my_group + step) % groups, member)

    w_copy = pltpu.make_async_copy(w_hbm.at[0], w, w_sem)
    w_copy.start()

    barrier = pltpu.get_barrier_semaphore()
    peers = [partner]
    peers += [z_peer(s, k) for s in range(1, nz) for k in range(2)]
    peers += [y_peer(s) for s in range(1, ny)]
    peers += [g_peer(s) for s in range(1, groups)]
    for peer in peers:
        pl.semaphore_signal(barrier, inc=1, device_id=peer, device_id_type=MESH)
    pl.semaphore_wait(barrier, len(peers))

    def push(src, dst, send_sem, recv_sem, peer):
        pltpu.make_async_remote_copy(
            src_ref=src, dst_ref=dst, send_sem=send_sem, recv_sem=recv_sem,
            device_id=peer, device_id_type=MESH,
        ).start()

    def columns(span):
        return pl.ds(span[0], span[1] - span[0])

    def flat(part):
        return pl.ds(part[0] * groups, (part[1] - part[0]) * groups)

    def block_of(ref, part, span):
        return ref[:, columns(part), columns(span)].reshape(flat(part).size, columns(span).size)

    for ch, span in enumerate(z_spans):
        cols = columns(span)
        place = buf.at[member, :, cols]
        sources = (tok_ref.at[:, cols], grad_ref.at[:, cols])
        for step in range(1, nz):
            for kind in range(2):
                push(sources[kind], place, z_send.at[ch], z_recv.at[ch], z_peer(step, kind))
        for kind in range(2):

            @pl.when(core == kind)
            def _():
                pltpu.make_async_copy(sources[kind], place, z_recv.at[ch]).start()
                push(sources[1 - kind], place, z_send.at[ch], z_recv.at[ch], partner)

    ids = ids_ref[...]
    weights = weights_ref[...]
    group_row = lax.broadcasted_iota(jnp.int32, (groups, tokens), 0)
    wanted = group_row * (ny * nz) + local
    hit = jnp.zeros((groups, tokens), F32)
    weight = jnp.zeros((groups, tokens), F32)
    for k in range(top):
        match = ids[k : k + 1, :] == wanted
        hit = hit + jnp.where(match, 1.0, 0.0)
        weight = weight + jnp.where(match, weights[k : k + 1, :], 0.0)
    before = lax.broadcasted_iota(jnp.int32, (tokens, tokens), 0) < lax.broadcasted_iota(
        jnp.int32, (tokens, tokens), 1
    )
    earlier = jnp.where(before, 1.0, 0.0).astype(BF16)
    rank = dot(hit.astype(BF16), earlier, ((1,), (0,)))
    limit = jnp.where(group_row == hot_ref[local], float(HOT_CAP), float(CAP))
    kept = (hit > 0.0) & (rank < limit)
    rank = jnp.where(kept, rank, -1.0)
    is_rows = core == 0
    gather_weight = jnp.where(is_rows, 1.0, weight)
    spread_weight = jnp.where(is_rows, weight, 1.0)
    slot = lax.broadcasted_iota(jnp.int32, (HOT_CAP, tokens), 0).astype(F32)
    for g in range(groups):
        one = jnp.where(rank[g : g + 1, :] == slot, 1.0, 0.0)
        factor = jnp.broadcast_to(
            jnp.sum(one * gather_weight[g : g + 1, :], axis=1, keepdims=True), (HOT_CAP, 128)
        )
        spread_one = one * spread_weight[g : g + 1, :]
        for low, high in both:
            at = pl.ds(low * groups + g * (high - low), high - low)
            pick[at, :] = one[low:high, :].astype(BF16)
            scale[at, :] = factor[low:high, :]
            acc[at, 0:tokens] = spread_one[low:high, :]
    turned = acc[:, 0:tokens].T
    spread[0] = turned.astype(BF16)
    spread[1] = (turned - turned.astype(BF16).astype(F32)).astype(BF16)

    def to_y(ch):
        mine = pl.ds(y * nz * 2, nz * 2)
        last = in_spans[ch][1]
        for zc, (a, b) in enumerate(z_spans):
            if a < last and zc not in z_done:
                z_done.append(zc)
                wait(buf.at[mine, :, columns((a, b))], z_recv.at[zc])
        block = buf.at[mine, :, columns(in_spans[ch])]
        for step in range(1, ny):
            push(block, block, y_send.at[ch], y_recv.at[ch], y_peer(step))

    def y_wait(ch):
        wait(buf.at[pl.ds(0, (ny - 1) * nz * 2), :, columns(in_spans[ch])], y_recv.at[ch])

    def to_owner(item):
        part, span = in_items[item]
        cols, slots_at, at = columns(span), columns(part), flat(part)
        width = cols.size
        block = buf[:, :, cols].astype(F32).reshape(tokens, width).astype(BF16)
        picked = dot(pick[at, :], block, ((1,), (0,))) * scale[at, 0:1]
        send[:, slots_at, cols] = picked.astype(BF16).reshape(groups, slots_at.size, width)
        place = rows.at[core, my_group, slots_at, cols]
        for step in range(1, groups):
            peer = g_peer(step)
            push(send.at[peer[0], slots_at, cols], place, g_send.at[item], g_recv.at[item], peer)
        pltpu.make_async_copy(send.at[my_group, slots_at, cols], place, g_recv.at[item]).start()

    def to_partner(item):
        part, span = in_items[item]
        block = rows.at[core, :, columns(part), columns(span)]
        wait(block, g_recv.at[item])
        push(block, block, f_send.at[item], f_recv.at[item], partner)

    def accumulate(item):
        part, span = in_items[item]
        at, to = columns(span), flat(part)
        wait(rows.at[1 - core, :, columns(part), at], f_recv.at[item])
        if item == 0:
            w_copy.wait()
        pre = dot(block_of(rows.at[0], part, span), w[at, 0 : 2 * half], ((1,), (0,)))
        down = dot(block_of(rows.at[1], part, span), w[at, 2 * half :], ((1,), (0,)))
        if span[0] == 0:
            acc[to, 0 : 2 * half] = pre
            acc[to, 2 * half :] = down
        else:
            acc[to, 0 : 2 * half] += pre
            acc[to, 2 * half :] += down

    def activate(part):
        size = part[1] - part[0]

        @pl.loop(0, groups)
        def _(g):
            at = pl.ds(pl.multiple_of(part[0] * groups + g * size, 16), size)
            gate = acc[at, 0:half]
            up = acc[at, half : 2 * half]
            d_hidden = acc[at, 2 * half :]
            sig = jax.nn.sigmoid(gate)
            active = gate * sig
            hid[at, :] = (active * up).astype(BF16)
            dab[at, 0:half] = (d_hidden * up * sig * (1.0 + gate * (1.0 - sig))).astype(BF16)
            dab[at, half:] = (d_hidden * active).astype(BF16)

    def results(item):
        part, span = out_items[item]
        at, to = columns(span), flat(part)
        outs = (
            dot(hid[to, :], w[at, 2 * half :], ((1,), (1,))).astype(BF16),
            dot(dab[to, :], w[at, 0 : 2 * half], ((1,), (1,))).astype(BF16),
        )
        for kind, value in enumerate(outs):
            for low, high in both:
                if part[0] <= low and high <= part[1]:
                    here = value[(low - part[0]) * groups : (high - part[0]) * groups, :]
                    pair[kind, :, low:high, at] = here.reshape(groups, high - low, at.size)
        rows_at = columns(part)
        push(
            pair.at[1 - core, :, rows_at, at], other.at[:, rows_at, at], h_send.at[item],
            h_recv.at[item], partner,
        )

    def to_origin(item):
        part, span = out_items[item]
        at, rows_at = columns(span), columns(part)
        wait(other.at[:, rows_at, at], h_recv.at[item])
        total[:, rows_at, at] = (
            pair[core, :, rows_at, at].astype(F32) + other[:, rows_at, at].astype(F32)
        ).astype(BF16)
        place = ret.at[my_group, rows_at, at]
        for step in range(1, groups):
            peer = g_peer(step)
            push(total.at[peer[0], rows_at, at], place, r_send.at[item], r_recv.at[item], peer)
        pltpu.make_async_copy(total.at[my_group, rows_at, at], place, r_recv.at[item]).start()

    def weight_part(ch):
        span = back_spans[ch]
        at = columns(span)
        for kind, grads, to in (
            (0, dab, pl.ds(0, 2 * half)), (1, hid, pl.ds(2 * half, half)),
        ):
            wg[0, at, to] = sum(
                dot(block_of(rows.at[kind], part, span), grads[flat(part), :], ((0,), (0,)))
                for part in both
            ).astype(BF16)

    def back_y(ch):
        span = back_spans[ch]
        at = columns(span)
        for item, (part, (low, high)) in enumerate(out_items):
            if low < span[1] and item not in arrived:
                arrived.append(item)
                wait(ret.at[:, columns(part), pl.ds(low, high - low)], r_recv.at[item])
        mixed = sum(
            dot(spread[piece, :, flat(part)], block_of(ret, part, span), ((1,), (0,)))
            for part in both
            for piece in range(2)
        )
        res[:, :, :, at] = mixed.astype(BF16).reshape(ny, nz, 16, at.size)
        place = yrecv.at[y, :, :, at]
        for step in range(1, ny):
            push(
                res.at[(y + step) % ny, :, :, at], place, ry_send.at[ch], ry_recv.at[ch],
                y_peer(step),
            )
        pltpu.make_async_copy(res.at[y, :, :, at], place, ry_recv.at[ch]).start()

    def back_z(ch):
        at = columns(back_spans[ch])
        wait(yrecv.at[:, :, :, at], ry_recv.at[ch])
        ysum[:, :, at] = jnp.sum(yrecv[:, :, :, at].astype(F32), axis=0).astype(BF16)
        place = zrecv.at[z, :, at]
        for step in range(1, nz):
            push(
                ysum.at[(z + step) % nz, :, at], place, rz_send.at[ch], rz_recv.at[ch],
                z_peer(step, core),
            )
        pltpu.make_async_copy(ysum.at[z, :, at], place, rz_recv.at[ch]).start()

    def finish(ch):
        at = columns(back_spans[ch])
        wait(zrecv.at[:, :, at], rz_recv.at[ch])
        done = jnp.sum(zrecv[:, :, at].astype(F32), axis=0)
        fin[:, :, at] = done.reshape(2, 8, at.size).astype(BF16)
        place = out_ref.at[core, :, at]
        push(fin.at[1 - core, :, at], place, o_send.at[ch], o_recv.at[ch], partner)
        pltpu.make_async_copy(fin.at[core, :, at], place, o_recv.at[ch]).start()

    z_done, arrived = [], []
    n_in, n_late, n_out, n_back = len(in_spans), len(late_spans), len(out_items), len(back_spans)
    for step in range(n_in + 1):
        if step < n_in:
            to_y(step)
        if step >= 1:
            y_wait(step - 1)
            to_owner(step - 1)
        if step >= 3:
            to_partner(step - 3)
            if step >= 4:
                accumulate(step - 4)
    for late in range(n_late):
        to_owner(n_in + late)
    for item in range(max(n_in - 2, 0), n_in):
        to_partner(item)
        accumulate(item - 1)
    accumulate(n_in - 1)
    activate(both[0])
    for item in range(EARLY):
        results(item)
        if item >= 1:
            to_origin(item - 1)
            if item - 1 < n_late:
                to_partner(n_in + item - 1)
    for late in range(EARLY - 1, n_late):
        to_partner(n_in + late)
    accumulate(n_in)
    to_origin(EARLY - 1)
    for late in range(1, n_late):
        accumulate(n_in + late)
    activate(both[1])
    results(EARLY)
    for item in range(EARLY + 1, n_out):
        results(item)
        to_origin(item - 1)
    weight_part(0)
    to_origin(n_out - 1)
    for step in range(n_back + 2):
        if step < n_back:
            if step + 1 < n_back:
                weight_part(step + 1)
            back_y(step)
        if 0 <= step - 1 < n_back:
            back_z(step - 1)
        if step >= 2:
            finish(step - 2)

    for ch, span in enumerate(z_spans):
        wait(buf.at[pl.ds(0, 2 * nz - 1), :, columns(span)], z_send.at[ch])
    for ch, span in enumerate(in_spans):
        wait(buf.at[pl.ds(0, (ny - 1) * nz * 2), :, columns(span)], y_send.at[ch])
    for item, (part, span) in enumerate(in_items):
        wait(send.at[pl.ds(0, groups - 1), columns(part), columns(span)], g_send.at[item])
        wait(rows.at[core, :, columns(part), columns(span)], f_send.at[item])
    for item, (part, span) in enumerate(out_items):
        wait(pair.at[1 - core, :, columns(part), columns(span)], h_send.at[item])
        wait(total.at[pl.ds(0, groups - 1), columns(part), columns(span)], r_send.at[item])
    for ch, span in enumerate(back_spans):
        at = columns(span)
        wait(res.at[pl.ds(0, ny - 1), :, :, at], ry_send.at[ch])
        wait(ysum.at[pl.ds(0, nz - 1), :, at], rz_send.at[ch])
        wait(fin.at[1 - core, :, at], o_send.at[ch])
        wait(fin.at[:, :, at], o_recv.at[ch])


def shards(ny, nz, tokens, expert_ids, combine, hot_group, expert_weights, out_grad):
    groups = lax.axis_size("group")
    chips = ny * nz
    rows_here, model_width = tokens.shape
    group_len = expert_ids.shape[0]
    hidden3 = expert_weights.shape[2]
    half = hidden3 // 3
    slots = groups * HOT_CAP
    dma = pltpu.SemaphoreType.DMA
    block = (groups, HOT_CAP, model_width)
    hbm = pl.BlockSpec(memory_space=pltpu.HBM)
    vmem = pl.BlockSpec(memory_space=pltpu.VMEM)
    n_z, n_y, n_in = len(Z_CUTS), len(IN_CUTS), len(IN_CUTS) + len(LATE_CUTS)
    n_out, n_back = len(OUT_CUTS) + 1, len(Y_CUTS)
    out, weight_grad = pl.pallas_call(
        functools.partial(layer, groups, ny, nz),
        out_shape=(
            pltpu.VMEM((2, rows_here, model_width), BF16),
            pltpu.VMEM(expert_weights.shape, BF16),
        ),
        in_specs=[
            pl.BlockSpec(memory_space=pltpu.SMEM), vmem, vmem, hbm, hbm, hbm,
        ],
        out_specs=(vmem, vmem),
        scratch_shapes=[
            pltpu.VMEM((model_width, hidden3), BF16),
            pltpu.VMEM((2 * chips, rows_here, model_width), BF16),
            pltpu.VMEM(block, BF16),
            pltpu.VMEM((2,) + block, BF16),
            pltpu.VMEM((slots, group_len), BF16),
            pltpu.VMEM((slots, 128), F32),
            pltpu.VMEM((2, group_len, slots), BF16),
            pltpu.VMEM((slots, hidden3), F32),
            pltpu.VMEM((slots, half), BF16),
            pltpu.VMEM((slots, 2 * half), BF16),
            pltpu.VMEM((2,) + block, BF16),
            pltpu.VMEM(block, BF16),
            pltpu.VMEM(block, BF16),
            pltpu.VMEM(block, BF16),
            pltpu.VMEM((ny, nz, 16, model_width), BF16),
            pltpu.VMEM((ny, nz, 16, model_width), BF16),
            pltpu.VMEM((nz, 16, model_width), BF16),
            pltpu.VMEM((nz, 16, model_width), BF16),
            pltpu.VMEM((2, rows_here, model_width), BF16),
            dma,
        ]
        + [dma((n_z,))] * 2
        + [dma((n_y,))] * 2
        + [dma((n_in,))] * 4
        + [dma((n_out,))] * 4
        + [dma((n_back,))] * 6,
        compiler_params=pltpu.CompilerParams(
            collective_id=0, has_side_effects=True, vmem_limit_bytes=VMEM_BYTES
        ),
        cost_estimate=pl.CostEstimate(
            flops=6 * slots * model_width * hidden3, bytes_accessed=4 * model_width * hidden3,
            transcendentals=slots * half,
        ),
    )(hot_group, expert_ids.T, combine.T, tokens, out_grad, expert_weights)
    return out[0], out[1], weight_grad


def solution(mesh):
    nz = 4 if mesh.shape["member"] == 32 else 2
    ny = mesh.shape["member"] // (2 * nz)
    return jax.shard_map(
        functools.partial(shards, ny, nz),
        mesh=mesh,
        in_specs=(
            P(("group", "member"), None),
            P("group", None),
            P("group", None),
            P(),
            P(("group", "member"), None, None),
            P(("group", "member"), None),
        ),
        out_specs=(
            P(("group", "member"), None),
            P(("group", "member"), None),
            P(("group", "member"), None, None),
        ),
        check_vma=False,
    )
```

```python
import functools

import jax
import jax.numpy as jnp
from jax import lax
from jax.experimental import pallas as pl
from jax.experimental.pallas import tpu as pltpu
from jax.sharding import PartitionSpec as P

MESH = pl.DeviceIdType.MESH
F32 = jnp.float32
BF16 = jnp.bfloat16
CAP = 24
HOT_CAP = 48
VMEM_BYTES = 56 * 2**20
Z_CUTS = (512, 512, 1024)
IN_CUTS = (512, 512, 512, 512)
LATE_CUTS = (1024, 1024)
OUT_CUTS = (512, 512, 512, 512)
Y_CUTS = (1024, 512, 512)
FIRST = 32
EARLY = 2


def spans(cuts, width):
    whole = sum(cuts)
    ends = [sum(cuts[: i + 1]) * width // whole for i in range(len(cuts))]
    return [(a, b) for a, b in zip([0] + ends[:-1], ends)]


def wait(ref, sem):
    pltpu.make_async_copy(ref, ref, sem).wait()


def dot(a, b, dims):
    return lax.dot_general(a, b, (dims, ((), ())), preferred_element_type=F32)


def layer(
    groups, ny, nz,
    hot_ref, ids_ref, weights_ref, tok_ref, grad_ref, w_hbm,
    out_ref, wg,
    w, buf, send, rows, pick, scale, spread, acc, hid, dab,
    pair, other, total, ret, res, yrecv, ysum, zrecv, fin,
    w_sem, z_send, z_recv, y_send, y_recv, g_send, g_recv, f_send, f_recv,
    h_send, h_recv, r_send, r_recv, ry_send, ry_recv, rz_send, rz_recv,
    o_send, o_recv,
):
    model_width = tok_ref.shape[1]
    z_spans = spans(Z_CUTS, model_width)
    in_spans = spans(IN_CUTS, model_width)
    late_spans = spans(LATE_CUTS, model_width)
    out_spans = spans(OUT_CUTS, model_width)
    back_spans = spans(Y_CUTS, model_width)
    both = ((0, FIRST), (FIRST, HOT_CAP))
    in_items = [(both[0], span) for span in in_spans] + [(both[1], span) for span in late_spans]
    out_items = [(both[0], span) for span in out_spans[:EARLY]]
    out_items += [(both[1], (0, out_spans[EARLY - 1][1]))]
    out_items += [((0, HOT_CAP), span) for span in out_spans[EARLY:]]
    top, tokens = ids_ref.shape
    slots = groups * HOT_CAP
    half = hid.shape[1]
    my_group = lax.axis_index("group")
    member = lax.axis_index("member")
    core = member % 2
    local = member // 2
    z = local % nz
    y = local // nz
    partner = (my_group, member + 1 - 2 * core)

    def z_peer(step, kind):
        return (my_group, (y * nz + (z + step) % nz) * 2 + kind)

    def y_peer(step):
        return (my_group, (((y + step) % ny) * nz + z) * 2 + core)

    def g_peer(step):
        return ((my_group + step) % groups, member)

    w_copy = pltpu.make_async_copy(w_hbm.at[0], w, w_sem)
    w_copy.start()

    barrier = pltpu.get_barrier_semaphore()
    peers = [partner]
    peers += [z_peer(s, k) for s in range(1, nz) for k in range(2)]
    peers += [y_peer(s) for s in range(1, ny)]
    peers += [g_peer(s) for s in range(1, groups)]
    for peer in peers:
        pl.semaphore_signal(barrier, inc=1, device_id=peer, device_id_type=MESH)
    pl.semaphore_wait(barrier, len(peers))

    def push(src, dst, send_sem, recv_sem, peer):
        pltpu.make_async_remote_copy(
            src_ref=src, dst_ref=dst, send_sem=send_sem, recv_sem=recv_sem,
            device_id=peer, device_id_type=MESH,
        ).start()

    def columns(span):
        return pl.ds(span[0], span[1] - span[0])

    def flat(part):
        return pl.ds(part[0] * groups, (part[1] - part[0]) * groups)

    def block_of(ref, part, span):
        return ref[:, columns(part), columns(span)].reshape(flat(part).size, columns(span).size)

    for ch, span in enumerate(z_spans):
        cols = columns(span)
        place = buf.at[member, :, cols]
        sources = (tok_ref.at[:, cols], grad_ref.at[:, cols])
        for step in range(1, nz):
            for kind in range(2):
                push(sources[kind], place, z_send, z_recv.at[ch], z_peer(step, kind))
        for kind in range(2):

            @pl.when(core == kind)
            def _():
                pltpu.make_async_copy(sources[kind], place, z_recv.at[ch]).start()
                push(sources[1 - kind], place, z_send, z_recv.at[ch], partner)

    ids = ids_ref[...]
    weights = weights_ref[...]
    group_row = lax.broadcasted_iota(jnp.int32, (groups, tokens), 0)
    wanted = group_row * (ny * nz) + local
    hit = jnp.zeros((groups, tokens), F32)
    weight = jnp.zeros((groups, tokens), F32)
    for k in range(top):
        match = ids[k : k + 1, :] == wanted
        hit = hit + jnp.where(match, 1.0, 0.0)
        weight = weight + jnp.where(match, weights[k : k + 1, :], 0.0)
    before = lax.broadcasted_iota(jnp.int32, (tokens, tokens), 0) < lax.broadcasted_iota(
        jnp.int32, (tokens, tokens), 1
    )
    earlier = jnp.where(before, 1.0, 0.0).astype(BF16)
    rank = dot(hit.astype(BF16), earlier, ((1,), (0,)))
    limit = jnp.where(group_row == hot_ref[local], float(HOT_CAP), float(CAP))
    kept = (hit > 0.0) & (rank < limit)
    rank = jnp.where(kept, rank, -1.0)
    is_rows = core == 0
    gather_weight = jnp.where(is_rows, 1.0, weight)
    spread_weight = jnp.where(is_rows, weight, 1.0)
    slot = lax.broadcasted_iota(jnp.int32, (HOT_CAP, tokens), 0).astype(F32)
    for g in range(groups):
        one = jnp.where(rank[g : g + 1, :] == slot, 1.0, 0.0)
        factor = jnp.broadcast_to(
            jnp.sum(one * gather_weight[g : g + 1, :], axis=1, keepdims=True), (HOT_CAP, 128)
        )
        spread_one = one * spread_weight[g : g + 1, :]
        for low, high in both:
            at = pl.ds(low * groups + g * (high - low), high - low)
            pick[at, :] = one[low:high, :].astype(BF16)
            scale[at, :] = factor[low:high, :]
            acc[at, 0:tokens] = spread_one[low:high, :]
    turned = acc[:, 0:tokens].T
    spread[0] = turned.astype(BF16)
    spread[1] = (turned - turned.astype(BF16).astype(F32)).astype(BF16)

    def to_y(ch):
        mine = pl.ds(y * nz * 2, nz * 2)
        last = in_spans[ch][1]
        for zc, (a, b) in enumerate(z_spans):
            if a < last and zc not in z_done:
                z_done.append(zc)
                wait(buf.at[mine, :, columns((a, b))], z_recv.at[zc])
        block = buf.at[mine, :, columns(in_spans[ch])]
        for step in range(1, ny):
            push(block, block, y_send, y_recv.at[ch], y_peer(step))

    def y_wait(ch):
        wait(buf.at[pl.ds(0, (ny - 1) * nz * 2), :, columns(in_spans[ch])], y_recv.at[ch])

    def to_owner(item):
        part, span = in_items[item]
        cols, slots_at, at = columns(span), columns(part), flat(part)
        width = cols.size
        block = buf[:, :, cols].astype(F32).reshape(tokens, width).astype(BF16)
        picked = dot(pick[at, :], block, ((1,), (0,))) * scale[at, 0:1]
        send[:, slots_at, cols] = picked.astype(BF16).reshape(groups, slots_at.size, width)
        place = rows.at[core, my_group, slots_at, cols]
        for step in range(1, groups):
            peer = g_peer(step)
            push(send.at[peer[0], slots_at, cols], place, g_send, g_recv.at[item], peer)
        pltpu.make_async_copy(send.at[my_group, slots_at, cols], place, g_recv.at[item]).start()

    def to_partner(item):
        part, span = in_items[item]
        block = rows.at[core, :, columns(part), columns(span)]
        wait(block, g_recv.at[item])
        push(block, block, f_send, f_recv.at[item], partner)

    def accumulate(item):
        part, span = in_items[item]
        at, to = columns(span), flat(part)
        wait(rows.at[1 - core, :, columns(part), at], f_recv.at[item])
        if item == 0:
            w_copy.wait()
        pre = dot(block_of(rows.at[0], part, span), w[at, 0 : 2 * half], ((1,), (0,)))
        down = dot(block_of(rows.at[1], part, span), w[at, 2 * half :], ((1,), (0,)))
        if span[0] == 0:
            acc[to, 0 : 2 * half] = pre
            acc[to, 2 * half :] = down
        else:
            acc[to, 0 : 2 * half] += pre
            acc[to, 2 * half :] += down

    def activate(part):
        size = part[1] - part[0]

        @pl.loop(0, groups)
        def _(g):
            at = pl.ds(pl.multiple_of(part[0] * groups + g * size, 16), size)
            gate = acc[at, 0:half]
            up = acc[at, half : 2 * half]
            d_hidden = acc[at, 2 * half :]
            sig = jax.nn.sigmoid(gate)
            active = gate * sig
            hid[at, :] = (active * up).astype(BF16)
            dab[at, 0:half] = (d_hidden * up * sig * (1.0 + gate * (1.0 - sig))).astype(BF16)
            dab[at, half:] = (d_hidden * active).astype(BF16)

    def results(item):
        part, span = out_items[item]
        at, to = columns(span), flat(part)
        outs = (
            dot(hid[to, :], w[at, 2 * half :], ((1,), (1,))).astype(BF16),
            dot(dab[to, :], w[at, 0 : 2 * half], ((1,), (1,))).astype(BF16),
        )
        for kind, value in enumerate(outs):
            for low, high in both:
                if part[0] <= low and high <= part[1]:
                    here = value[(low - part[0]) * groups : (high - part[0]) * groups, :]
                    pair[kind, :, low:high, at] = here.reshape(groups, high - low, at.size)
        rows_at = columns(part)
        push(
            pair.at[1 - core, :, rows_at, at], other.at[:, rows_at, at], h_send,
            h_recv.at[item], partner,
        )

    def to_origin(item):
        part, span = out_items[item]
        at, rows_at = columns(span), columns(part)
        wait(other.at[:, rows_at, at], h_recv.at[item])
        total[:, rows_at, at] = (
            pair[core, :, rows_at, at].astype(F32) + other[:, rows_at, at].astype(F32)
        ).astype(BF16)
        place = ret.at[my_group, rows_at, at]
        for step in range(1, groups):
            peer = g_peer(step)
            push(total.at[peer[0], rows_at, at], place, r_send, r_recv.at[item], peer)
        pltpu.make_async_copy(total.at[my_group, rows_at, at], place, r_recv.at[item]).start()

    def weight_part(ch):
        span = back_spans[ch]
        at = columns(span)
        for kind, grads, to in (
            (0, dab, pl.ds(0, 2 * half)), (1, hid, pl.ds(2 * half, half)),
        ):
            wg[0, at, to] = sum(
                dot(block_of(rows.at[kind], part, span), grads[flat(part), :], ((0,), (0,)))
                for part in both
            ).astype(BF16)

    def back_y(ch):
        span = back_spans[ch]
        at = columns(span)
        for item, (part, (low, high)) in enumerate(out_items):
            if low < span[1] and item not in arrived:
                arrived.append(item)
                wait(ret.at[:, columns(part), pl.ds(low, high - low)], r_recv.at[item])
        mixed = sum(
            dot(spread[piece, :, flat(part)], block_of(ret, part, span), ((1,), (0,)))
            for part in both
            for piece in range(2)
        )
        res[:, :, :, at] = mixed.astype(BF16).reshape(ny, nz, 16, at.size)
        place = yrecv.at[y, :, :, at]
        for step in range(1, ny):
            push(
                res.at[(y + step) % ny, :, :, at], place, ry_send, ry_recv.at[ch],
                y_peer(step),
            )
        pltpu.make_async_copy(res.at[y, :, :, at], place, ry_recv.at[ch]).start()

    def back_z(ch):
        at = columns(back_spans[ch])
        wait(yrecv.at[:, :, :, at], ry_recv.at[ch])
        ysum[:, :, at] = jnp.sum(yrecv[:, :, :, at].astype(F32), axis=0).astype(BF16)
        place = zrecv.at[z, :, at]
        for step in range(1, nz):
            push(
                ysum.at[(z + step) % nz, :, at], place, rz_send, rz_recv.at[ch],
                z_peer(step, core),
            )
        pltpu.make_async_copy(ysum.at[z, :, at], place, rz_recv.at[ch]).start()

    def finish(ch):
        at = columns(back_spans[ch])
        wait(zrecv.at[:, :, at], rz_recv.at[ch])
        done = jnp.sum(zrecv[:, :, at].astype(F32), axis=0)
        fin[:, :, at] = done.reshape(2, 8, at.size).astype(BF16)
        place = out_ref.at[core, :, at]
        push(fin.at[1 - core, :, at], place, o_send, o_recv, partner)
        pltpu.make_async_copy(fin.at[core, :, at], place, o_recv).start()

    z_done, arrived = [], []
    n_in, n_late, n_out, n_back = len(in_spans), len(late_spans), len(out_items), len(back_spans)
    for ch in range(n_in):
        to_y(ch)
    for ch in range(n_in):
        y_wait(ch)
        to_owner(ch)
        if ch == n_in - 1:
            for late in range(n_late):
                to_owner(n_in + late)
        if ch >= 2:
            to_partner(ch - 2)
    for item in range(n_in - 2):
        accumulate(item)
    to_partner(n_in - 2)
    to_partner(n_in - 1)
    accumulate(n_in - 2)
    accumulate(n_in - 1)
    activate(both[0])
    results(0)
    for item in range(1, EARLY):
        results(item)
        to_origin(item - 1)
    to_origin(EARLY - 1)
    for late in range(n_late):
        to_partner(n_in + late)
        if late >= 1:
            accumulate(n_in + late - 1)
    accumulate(n_in + n_late - 1)
    activate(both[1])
    results(EARLY)
    for item in range(EARLY + 1, n_out):
        results(item)
        to_origin(item - 1)
    weight_part(0)
    to_origin(n_out - 1)
    for ch in range(n_back):
        if ch + 1 < n_back:
            weight_part(ch + 1)
        back_y(ch)
    for ch in range(n_back):
        back_z(ch)
    for ch in range(n_back):
        finish(ch)

    wait(buf.at[pl.ds(0, 2 * nz - 1)], z_send)
    wait(buf.at[pl.ds(0, (ny - 1) * nz * 2)], y_send)
    wait(send.at[pl.ds(0, groups - 1)], g_send)
    wait(rows.at[core], f_send)
    wait(pair.at[1 - core], h_send)
    wait(total.at[pl.ds(0, groups - 1)], r_send)
    wait(res.at[pl.ds(0, ny - 1)], ry_send)
    wait(ysum.at[pl.ds(0, nz - 1)], rz_send)
    wait(fin.at[1 - core], o_send)
    wait(fin, o_recv)


def shards(ny, nz, tokens, expert_ids, combine, hot_group, expert_weights, out_grad):
    groups = lax.axis_size("group")
    chips = ny * nz
    rows_here, model_width = tokens.shape
    group_len = expert_ids.shape[0]
    hidden3 = expert_weights.shape[2]
    half = hidden3 // 3
    slots = groups * HOT_CAP
    dma = pltpu.SemaphoreType.DMA
    block = (groups, HOT_CAP, model_width)
    hbm = pl.BlockSpec(memory_space=pltpu.HBM)
    vmem = pl.BlockSpec(memory_space=pltpu.VMEM)
    n_z, n_y, n_in = len(Z_CUTS), len(IN_CUTS), len(IN_CUTS) + len(LATE_CUTS)
    n_out, n_back = len(OUT_CUTS) + 1, len(Y_CUTS)
    out, weight_grad = pl.pallas_call(
        functools.partial(layer, groups, ny, nz),
        out_shape=(
            pltpu.VMEM((2, rows_here, model_width), BF16),
            pltpu.VMEM(expert_weights.shape, BF16),
        ),
        in_specs=[
            pl.BlockSpec(memory_space=pltpu.SMEM), vmem, vmem, hbm, hbm, hbm,
        ],
        out_specs=(vmem, vmem),
        scratch_shapes=[
            pltpu.VMEM((model_width, hidden3), BF16),
            pltpu.VMEM((2 * chips, rows_here, model_width), BF16),
            pltpu.VMEM(block, BF16),
            pltpu.VMEM((2,) + block, BF16),
            pltpu.VMEM((slots, group_len), BF16),
            pltpu.VMEM((slots, 128), F32),
            pltpu.VMEM((2, group_len, slots), BF16),
            pltpu.VMEM((slots, hidden3), F32),
            pltpu.VMEM((slots, half), BF16),
            pltpu.VMEM((slots, 2 * half), BF16),
            pltpu.VMEM((2,) + block, BF16),
            pltpu.VMEM(block, BF16),
            pltpu.VMEM(block, BF16),
            pltpu.VMEM(block, BF16),
            pltpu.VMEM((ny, nz, 16, model_width), BF16),
            pltpu.VMEM((ny, nz, 16, model_width), BF16),
            pltpu.VMEM((nz, 16, model_width), BF16),
            pltpu.VMEM((nz, 16, model_width), BF16),
            pltpu.VMEM((2, rows_here, model_width), BF16),
            dma,
        ]
        + [dma, dma((n_z,)), dma, dma((n_y,))]
        + [dma, dma((n_in,))] * 2
        + [dma, dma((n_out,))] * 2
        + [dma, dma((n_back,))] * 2
        + [dma, dma],
        compiler_params=pltpu.CompilerParams(
            collective_id=0, has_side_effects=True, vmem_limit_bytes=VMEM_BYTES
        ),
        cost_estimate=pl.CostEstimate(
            flops=6 * slots * model_width * hidden3, bytes_accessed=4 * model_width * hidden3,
            transcendentals=slots * half,
        ),
    )(hot_group, expert_ids.T, combine.T, tokens, out_grad, expert_weights)
    return out[0], out[1], weight_grad


def solution(mesh):
    nz = 4 if mesh.shape["member"] == 32 else 2
    ny = mesh.shape["member"] // (2 * nz)
    return jax.shard_map(
        functools.partial(shards, ny, nz),
        mesh=mesh,
        in_specs=(
            P(("group", "member"), None),
            P("group", None),
            P("group", None),
            P(),
            P(("group", "member"), None, None),
            P(("group", "member"), None),
        ),
        out_specs=(
            P(("group", "member"), None),
            P(("group", "member"), None),
            P(("group", "member"), None, None),
        ),
        check_vma=False,
    )
```

```python
import functools

import jax
import jax.numpy as jnp
from jax import lax
from jax.experimental import pallas as pl
from jax.experimental.pallas import tpu as pltpu
from jax.sharding import PartitionSpec as P

MESH = pl.DeviceIdType.MESH
F32 = jnp.float32
BF16 = jnp.bfloat16
CAP = 24
HOT_CAP = 48
VMEM_BYTES = 56 * 2**20
Z_CUTS = (512, 1536)
IN_CUTS = (512, 512, 512, 512)
LATE_CUTS = (1024, 1024)
OUT_CUTS = (512, 512, 512, 512)
Y_CUTS = (512, 512, 512, 512)
FIRST = 32
EARLY = 2


def spans(cuts, width):
    whole = sum(cuts)
    ends = [sum(cuts[: i + 1]) * width // whole for i in range(len(cuts))]
    return [(a, b) for a, b in zip([0] + ends[:-1], ends)]


def wait(ref, sem):
    pltpu.make_async_copy(ref, ref, sem).wait()


def dot(a, b, dims):
    return lax.dot_general(a, b, (dims, ((), ())), preferred_element_type=F32)


def layer(
    groups, ny, nz,
    hot_ref, ids_ref, weights_ref, tok_ref, grad_ref, w_hbm,
    out_ref, wg,
    w, buf, send, rows, pick, scale, spread, acc, hid, dab,
    pair, other, total, ret, res, yrecv, ysum, zrecv,
    w_sem, z_send, z_recv, y_send, y_recv, g_send, g_recv, f_send, f_recv,
    h_send, h_recv, r_send, r_recv, ry_send, ry_recv, rz_send, rz_recv,
):
    model_width = tok_ref.shape[1]
    z_spans = spans(Z_CUTS, model_width)
    in_spans = spans(IN_CUTS, model_width)
    late_spans = spans(LATE_CUTS, model_width)
    out_spans = spans(OUT_CUTS, model_width)
    back_spans = spans(Y_CUTS, model_width)
    both = ((0, FIRST), (FIRST, HOT_CAP))
    in_items = [(both[0], span) for span in in_spans] + [(both[1], span) for span in late_spans]
    out_items = [(both[0], span) for span in out_spans[:EARLY]]
    out_items += [(both[1], (0, out_spans[EARLY - 1][1]))]
    out_items += [((0, HOT_CAP), span) for span in out_spans[EARLY:]]
    top, tokens = ids_ref.shape
    slots = groups * HOT_CAP
    half = hid.shape[1]
    my_group = lax.axis_index("group")
    member = lax.axis_index("member")
    core = member % 2
    local = member // 2
    z = local % nz
    y = local // nz
    partner = (my_group, member + 1 - 2 * core)

    def z_peer(step, kind):
        return (my_group, (y * nz + (z + step) % nz) * 2 + kind)

    def y_peer(step):
        return (my_group, (((y + step) % ny) * nz + z) * 2 + core)

    def g_peer(step):
        return ((my_group + step) % groups, member)

    w_copy = pltpu.make_async_copy(w_hbm.at[0], w, w_sem)
    w_copy.start()

    barrier = pltpu.get_barrier_semaphore()
    peers = [partner]
    peers += [z_peer(s, k) for s in range(1, nz) for k in range(2)]
    peers += [y_peer(s) for s in range(1, ny)]
    peers += [g_peer(s) for s in range(1, groups)]
    for peer in peers:
        pl.semaphore_signal(barrier, inc=1, device_id=peer, device_id_type=MESH)
    pl.semaphore_wait(barrier, len(peers))

    def push(src, dst, send_sem, recv_sem, peer):
        pltpu.make_async_remote_copy(
            src_ref=src, dst_ref=dst, send_sem=send_sem, recv_sem=recv_sem,
            device_id=peer, device_id_type=MESH,
        ).start()

    def columns(span):
        return pl.ds(span[0], span[1] - span[0])

    def flat(part):
        return pl.ds(part[0] * groups, (part[1] - part[0]) * groups)

    def block_of(ref, part, span):
        return ref[:, columns(part), columns(span)].reshape(flat(part).size, columns(span).size)

    for ch, span in enumerate(z_spans):
        cols = columns(span)
        place = buf.at[member, :, cols]
        sources = (tok_ref.at[:, cols], grad_ref.at[:, cols])
        for step in range(1, nz):
            for kind in range(2):
                push(sources[kind], place, z_send, z_recv.at[ch], z_peer(step, kind))
        for kind in range(2):

            @pl.when(core == kind)
            def _():
                pltpu.make_async_copy(sources[kind], place, z_recv.at[ch]).start()
                push(sources[1 - kind], place, z_send, z_recv.at[ch], partner)

    ids = ids_ref[...]
    weights = weights_ref[...]
    group_row = lax.broadcasted_iota(jnp.int32, (groups, tokens), 0)
    wanted = group_row * (ny * nz) + local
    hit = jnp.zeros((groups, tokens), F32)
    weight = jnp.zeros((groups, tokens), F32)
    for k in range(top):
        match = ids[k : k + 1, :] == wanted
        hit = hit + jnp.where(match, 1.0, 0.0)
        weight = weight + jnp.where(match, weights[k : k + 1, :], 0.0)
    before = lax.broadcasted_iota(jnp.int32, (tokens, tokens), 0) < lax.broadcasted_iota(
        jnp.int32, (tokens, tokens), 1
    )
    earlier = jnp.where(before, 1.0, 0.0).astype(BF16)
    rank = dot(hit.astype(BF16), earlier, ((1,), (0,)))
    limit = jnp.where(group_row == hot_ref[local], float(HOT_CAP), float(CAP))
    kept = (hit > 0.0) & (rank < limit)
    rank = jnp.where(kept, rank, -1.0)
    is_rows = core == 0
    gather_weight = jnp.where(is_rows, 1.0, weight)
    spread_weight = jnp.where(is_rows, weight, 1.0)
    slot = lax.broadcasted_iota(jnp.int32, (HOT_CAP, tokens), 0).astype(F32)
    for g in range(groups):
        one = jnp.where(rank[g : g + 1, :] == slot, 1.0, 0.0)
        factor = jnp.broadcast_to(
            jnp.sum(one * gather_weight[g : g + 1, :], axis=1, keepdims=True), (HOT_CAP, 128)
        )
        spread_one = one * spread_weight[g : g + 1, :]
        for low, high in both:
            at = pl.ds(low * groups + g * (high - low), high - low)
            pick[at, :] = one[low:high, :].astype(BF16)
            scale[at, :] = factor[low:high, :]
            acc[at, 0:tokens] = spread_one[low:high, :]
    turned = acc[:, 0:tokens].T
    spread[0] = turned.astype(BF16)
    spread[1] = (turned - turned.astype(BF16).astype(F32)).astype(BF16)

    def to_y(ch):
        mine = pl.ds(y * nz * 2, nz * 2)
        last = in_spans[ch][1]
        for zc, (a, b) in enumerate(z_spans):
            if a < last and zc not in z_done:
                z_done.append(zc)
                wait(buf.at[mine, :, columns((a, b))], z_recv.at[zc])
        block = buf.at[mine, :, columns(in_spans[ch])]
        for step in range(1, ny):
            push(block, block, y_send, y_recv.at[ch], y_peer(step))

    def y_wait(ch):
        wait(buf.at[pl.ds(0, (ny - 1) * nz * 2), :, columns(in_spans[ch])], y_recv.at[ch])

    def to_owner(item):
        part, span = in_items[item]
        cols, slots_at, at = columns(span), columns(part), flat(part)
        width = cols.size
        block = buf[:, :, cols].astype(F32).reshape(tokens, width).astype(BF16)
        picked = dot(pick[at, :], block, ((1,), (0,))) * scale[at, 0:1]
        send[:, slots_at, cols] = picked.astype(BF16).reshape(groups, slots_at.size, width)
        place = rows.at[core, my_group, slots_at, cols]
        for step in range(1, groups):
            peer = g_peer(step)
            push(send.at[peer[0], slots_at, cols], place, g_send, g_recv.at[item], peer)
        pltpu.make_async_copy(send.at[my_group, slots_at, cols], place, g_recv.at[item]).start()

    def to_partner(item):
        part, span = in_items[item]
        block = rows.at[core, :, columns(part), columns(span)]
        wait(block, g_recv.at[item])
        push(block, block, f_send, f_recv.at[item], partner)

    def accumulate(item):
        part, span = in_items[item]
        at, to = columns(span), flat(part)
        wait(rows.at[1 - core, :, columns(part), at], f_recv.at[item])
        if item == 0:
            w_copy.wait()
        pre = dot(block_of(rows.at[0], part, span), w[at, 0 : 2 * half], ((1,), (0,)))
        down = dot(block_of(rows.at[1], part, span), w[at, 2 * half :], ((1,), (0,)))
        if span[0] == 0:
            acc[to, 0 : 2 * half] = pre
            acc[to, 2 * half :] = down
        else:
            acc[to, 0 : 2 * half] += pre
            acc[to, 2 * half :] += down

    def activate(part):
        size = part[1] - part[0]

        @pl.loop(0, groups)
        def _(g):
            at = pl.ds(pl.multiple_of(part[0] * groups + g * size, 16), size)
            gate = acc[at, 0:half]
            up = acc[at, half : 2 * half]
            d_hidden = acc[at, 2 * half :]
            sig = jax.nn.sigmoid(gate)
            active = gate * sig
            hid[at, :] = (active * up).astype(BF16)
            dab[at, 0:half] = (d_hidden * up * sig * (1.0 + gate * (1.0 - sig))).astype(BF16)
            dab[at, half:] = (d_hidden * active).astype(BF16)

    def results(item):
        part, span = out_items[item]
        at, to = columns(span), flat(part)
        outs = (
            dot(hid[to, :], w[at, 2 * half :], ((1,), (1,))).astype(BF16),
            dot(dab[to, :], w[at, 0 : 2 * half], ((1,), (1,))).astype(BF16),
        )
        for kind, value in enumerate(outs):
            for low, high in both:
                if part[0] <= low and high <= part[1]:
                    here = value[(low - part[0]) * groups : (high - part[0]) * groups, :]
                    pair[kind, :, low:high, at] = here.reshape(groups, high - low, at.size)
        rows_at = columns(part)
        push(
            pair.at[1 - core, :, rows_at, at], other.at[:, rows_at, at], h_send,
            h_recv.at[item], partner,
        )

    def to_origin(item):
        part, span = out_items[item]
        at, rows_at = columns(span), columns(part)
        wait(other.at[:, rows_at, at], h_recv.at[item])
        total[:, rows_at, at] = (
            pair[core, :, rows_at, at].astype(F32) + other[:, rows_at, at].astype(F32)
        ).astype(BF16)
        place = ret.at[my_group, rows_at, at]
        for step in range(1, groups):
            peer = g_peer(step)
            push(total.at[peer[0], rows_at, at], place, r_send, r_recv.at[item], peer)
        pltpu.make_async_copy(total.at[my_group, rows_at, at], place, r_recv.at[item]).start()

    def weight_part(ch):
        span = back_spans[ch]
        at = columns(span)
        for kind, grads, to in (
            (0, dab, pl.ds(0, 2 * half)), (1, hid, pl.ds(2 * half, half)),
        ):
            wg[0, at, to] = sum(
                dot(block_of(rows.at[kind], part, span), grads[flat(part), :], ((0,), (0,)))
                for part in both
            ).astype(BF16)

    def back_y(ch):
        span = back_spans[ch]
        at = columns(span)
        for item, (part, (low, high)) in enumerate(out_items):
            if low < span[1] and item not in arrived:
                arrived.append(item)
                wait(ret.at[:, columns(part), pl.ds(low, high - low)], r_recv.at[item])
        mixed = sum(
            dot(spread[piece, :, flat(part)], block_of(ret, part, span), ((1,), (0,)))
            for part in both
            for piece in range(2)
        )
        res[:, :, :, at] = mixed.astype(BF16).reshape(ny, nz, 16, at.size)
        place = yrecv.at[y, :, :, at]
        for step in range(1, ny):
            push(
                res.at[(y + step) % ny, :, :, at], place, ry_send, ry_recv.at[ch],
                y_peer(step),
            )
        pltpu.make_async_copy(res.at[y, :, :, at], place, ry_recv.at[ch]).start()

    def back_z(ch):
        at = columns(back_spans[ch])
        wait(yrecv.at[:, :, :, at], ry_recv.at[ch])
        summed = jnp.sum(yrecv[:, :, :, at].astype(F32), axis=0)
        ysum[:, :, at] = summed.reshape(2 * nz, 8, at.size).astype(BF16)
        place = zrecv.at[core, z, :, at]
        for step in range(1, nz):
            for k in range(2):
                piece = ysum.at[(z + step) % nz * 2 + k, :, at]
                push(piece, place, rz_send, rz_recv.at[ch], z_peer(step, k))
        push(ysum.at[2 * z + 1 - core, :, at], place, rz_send, rz_recv.at[ch], partner)
        pltpu.make_async_copy(ysum.at[2 * z + core, :, at], place, rz_recv.at[ch]).start()

    def finish(ch):
        at = columns(back_spans[ch])
        wait(zrecv.at[:, :, :, at], rz_recv.at[ch])
        out_ref[:, :, at] = jnp.sum(zrecv[:, :, :, at].astype(F32), axis=1).astype(BF16)

    z_done, arrived = [], []
    n_in, n_late, n_out, n_back = len(in_spans), len(late_spans), len(out_items), len(back_spans)
    for ch in range(n_in):
        to_y(ch)
    for ch in range(n_in):
        y_wait(ch)
        to_owner(ch)
        if ch == n_in - 1:
            for late in range(n_late):
                to_owner(n_in + late)
        if ch >= 2:
            to_partner(ch - 2)
    for item in range(n_in - 2):
        accumulate(item)
    to_partner(n_in - 2)
    to_partner(n_in - 1)
    accumulate(n_in - 2)
    accumulate(n_in - 1)
    activate(both[0])
    results(0)
    for item in range(1, EARLY):
        results(item)
        to_origin(item - 1)
    to_origin(EARLY - 1)
    for late in range(n_late):
        to_partner(n_in + late)
        if late >= 1:
            accumulate(n_in + late - 1)
    accumulate(n_in + n_late - 1)
    activate(both[1])
    results(EARLY)
    for item in range(EARLY + 1, n_out):
        results(item)
        to_origin(item - 1)
    weight_part(0)
    to_origin(n_out - 1)
    for ch in range(n_back):
        if ch + 1 < n_back:
            weight_part(ch + 1)
        back_y(ch)
    for ch in range(n_back):
        back_z(ch)
    for ch in range(n_back):
        finish(ch)

    wait(buf.at[pl.ds(0, 2 * nz - 1)], z_send)
    wait(buf.at[pl.ds(0, (ny - 1) * nz * 2)], y_send)
    wait(send.at[pl.ds(0, groups - 1)], g_send)
    wait(rows.at[core], f_send)
    wait(pair.at[1 - core], h_send)
    wait(total.at[pl.ds(0, groups - 1)], r_send)
    wait(res.at[pl.ds(0, ny - 1)], ry_send)
    wait(ysum.at[pl.ds(0, 2 * nz - 1)], rz_send)


def shards(ny, nz, tokens, expert_ids, combine, hot_group, expert_weights, out_grad):
    groups = lax.axis_size("group")
    chips = ny * nz
    rows_here, model_width = tokens.shape
    group_len = expert_ids.shape[0]
    hidden3 = expert_weights.shape[2]
    half = hidden3 // 3
    slots = groups * HOT_CAP
    dma = pltpu.SemaphoreType.DMA
    block = (groups, HOT_CAP, model_width)
    hbm = pl.BlockSpec(memory_space=pltpu.HBM)
    vmem = pl.BlockSpec(memory_space=pltpu.VMEM)
    n_z, n_y, n_in = len(Z_CUTS), len(IN_CUTS), len(IN_CUTS) + len(LATE_CUTS)
    n_out, n_back = len(OUT_CUTS) + 1, len(Y_CUTS)
    out, weight_grad = pl.pallas_call(
        functools.partial(layer, groups, ny, nz),
        out_shape=(
            pltpu.VMEM((2, rows_here, model_width), BF16),
            pltpu.VMEM(expert_weights.shape, BF16),
        ),
        in_specs=[
            pl.BlockSpec(memory_space=pltpu.SMEM), vmem, vmem, hbm, hbm, hbm,
        ],
        out_specs=(vmem, vmem),
        scratch_shapes=[
            pltpu.VMEM((model_width, hidden3), BF16),
            pltpu.VMEM((2 * chips, rows_here, model_width), BF16),
            pltpu.VMEM(block, BF16),
            pltpu.VMEM((2,) + block, BF16),
            pltpu.VMEM((slots, group_len), BF16),
            pltpu.VMEM((slots, 128), F32),
            pltpu.VMEM((2, group_len, slots), BF16),
            pltpu.VMEM((slots, hidden3), F32),
            pltpu.VMEM((slots, half), BF16),
            pltpu.VMEM((slots, 2 * half), BF16),
            pltpu.VMEM((2,) + block, BF16),
            pltpu.VMEM(block, BF16),
            pltpu.VMEM(block, BF16),
            pltpu.VMEM(block, BF16),
            pltpu.VMEM((ny, nz, 16, model_width), BF16),
            pltpu.VMEM((ny, nz, 16, model_width), BF16),
            pltpu.VMEM((2 * nz, 8, model_width), BF16),
            pltpu.VMEM((2, nz, 8, model_width), BF16),
            dma,
        ]
        + [dma, dma((n_z,)), dma, dma((n_y,))]
        + [dma, dma((n_in,))] * 2
        + [dma, dma((n_out,))] * 2
        + [dma, dma((n_back,))] * 2,
        compiler_params=pltpu.CompilerParams(
            collective_id=0, has_side_effects=True, vmem_limit_bytes=VMEM_BYTES
        ),
        cost_estimate=pl.CostEstimate(
            flops=6 * slots * model_width * hidden3, bytes_accessed=4 * model_width * hidden3,
            transcendentals=slots * half,
        ),
    )(hot_group, expert_ids.T, combine.T, tokens, out_grad, expert_weights)
    return out[0], out[1], weight_grad


def solution(mesh):
    nz = 4 if mesh.shape["member"] == 32 else 2
    ny = mesh.shape["member"] // (2 * nz)
    return jax.shard_map(
        functools.partial(shards, ny, nz),
        mesh=mesh,
        in_specs=(
            P(("group", "member"), None),
            P("group", None),
            P("group", None),
            P(),
            P(("group", "member"), None, None),
            P(("group", "member"), None),
        ),
        out_specs=(
            P(("group", "member"), None),
            P(("group", "member"), None),
            P(("group", "member"), None, None),
        ),
        check_vma=False,
    )
```
